32 devices in a mesh: groups: 2 (over y), tensor: 4 (over z), expert: 4 (over x, core).
Axes of the slice: x: 2, y: 2, z: 4, core: 2. Of those that a mesh axis runs over, the one named last changes fastest.
Arguments:
- tokens: bfloat16 [1024, 3072], P(('groups', 'expert'), 'tensor'), parts along dimension 0, may hold values from -6 to 6
- expert_ids: int32 [1024, 2], P(('groups', 'expert')), parts along dimension 0, may hold values from 0 to 7, all different within a row; in each aligned block of 128 rows (0 to 127, 128 to 255, ...) at most 64 rows name the same one
- router_logits: float32 [1024, 2], P(('groups', 'expert')), parts along dimension 0, may hold values from -6 to 6
- gate_weight: bfloat16 [8, 3072, 8192], P('expert', None, 'tensor'), may hold values from -0.109375 to 0.109375
- up_weight: bfloat16 [8, 3072, 8192], P('expert', None, 'tensor'), may hold values from -0.109375 to 0.109375
- down_weight: bfloat16 [8, 8192, 3072], P('expert', 'tensor'), may hold values from -0.0625 to 0.0625
Outputs:
- mixed: bfloat16 [1024, 3072], P(('groups', 'expert'), 'tensor'), parts along dimension 0
The draws below stay inside these ranges and needn't reach their ends.
There are 2 independent parts, one for each index of `groups`. The reference program is written for one: setup_inputs(seed, part) draws one part's arguments, and reference() takes and returns one part's arrays. A program takes and returns all parts, laid end to end along the dimension named above; an argument that names none is the same for every part. Nothing has to cross between parts.
Inputs may be any that keep to these rules, and one draw needn't show every extreme that they name: `expert_ids`: each row names two different experts. In each aligned block of 128 rows (the rows of one index of expert) no expert is named more than 64 times, a bound that some block reaches.
All inputs are finite; a program needn't handle non-finite values.
Results may differ from the reference program's by a relative error of at most 0.01.
Values may be sent and summed in bfloat16 or wider, within the bound.
A program may use at most 192 MiB of HBM per device.

```python
import math
import jax
import jax.numpy as jnp
import numpy as np
from jax import lax

D = 3072
FF = 8192
EXPERTS = 8
TOK_DEV = 128
CAP = 64
TOKENS = 512
N_TENSOR = 4
N_EXPERT = 4


def shard_levels(stream_key, dims, split, smallest, high):
    loudness = 1.0
    for axis_at, parts in split:
        heights = jax.random.uniform(jax.random.fold_in(jax.random.fold_in(stream_key, 6), axis_at), (parts,), jnp.float32, smallest / len(split), high / len(split))
        loudness = loudness * jnp.repeat(jnp.exp(heights), dims[axis_at] // parts).reshape((-1,) + (1,) * (len(dims) - 1 - axis_at))
    return loudness


def routed_block(rng, own, number, rows, amount, top, reach, slope):
    order = jax.random.permutation(rng, amount)
    heavy_load, common = portions_of(amount, rows * top, reach, slope, True), portions_of(amount, rows * top, reach, slope, False)
    places = jnp.arange(amount)

    def named(sizes, turn):
        used = int((sizes > 0).sum())
        fixed = max(1, used // 4)
        shifted = fixed + (places - fixed + turn * (used - fixed)) % max(1, amount - fixed)
        return jnp.zeros((amount,), jnp.int32).at[order[jnp.where(places < fixed, places, shifted)]].set(jnp.asarray(sizes, jnp.int32))

    sizes = jnp.where(number % 4 == 0, named(heavy_load, number // 4), named(common, number - number // 4 - 1))
    mixed = jax.random.permutation(jax.random.fold_in(own, 3), amount)
    source_of, taker = mixed[0:amount // 2 * 2:2], mixed[1:amount // 2 * 2:2]
    margin = jnp.minimum(sizes[source_of] - 1, reach - sizes[taker]) // 2
    margin = jnp.where((source_of == order[0]) | (taker == order[0]) | (sizes[taker] == 0), 0, jnp.maximum(margin, 0))
    shifted = jax.random.randint(jax.random.fold_in(own, 4), (amount // 2,), 0, 1 << 20) % (margin + 1)
    sizes = sizes.at[source_of].add(-shifted).at[taker].add(shifted)
    labels = jnp.searchsorted(jnp.cumsum(sizes), jnp.arange(rows * top), side="right").astype(jnp.int32)
    table = labels.reshape(top, rows).T
    table = table[jax.random.permutation(jax.random.fold_in(own, 1), rows)]
    turn = jax.random.randint(jax.random.fold_in(own, 2), (rows, 1), 0, top)
    return jnp.take_along_axis(table, (jnp.arange(top)[None, :] + turn) % top, axis=1)


def portions_of(number_of, total, reach, lean, full):
    weights = [(1 << 20) // math.isqrt(rank ** lean) + 1 for rank in range(1, number_of + 1)]
    largest = reach if full else min(reach, max(-(-total // number_of), total * weights[0] // sum(weights)))
    least = 1 if total - largest >= number_of - 1 else 0
    counts, spare = [largest] + [least] * (number_of - 1), total - largest - least * (number_of - 1)
    while spare > 0:
        free = [i for i in range(1, number_of) if counts[i] < largest] or [i for i in range(1, number_of) if counts[i] < reach]
        whole, left = sum([weights[i] for i in free]), spare
        for i in free:
            addition = min(reach - counts[i], max(1, left * weights[i] // whole), spare)
            counts[i] = counts[i] + addition
            spare = spare - addition
    return np.array(counts)


def bell_draw(rng, dims, width, limit, cuts=(), kind=jnp.bfloat16):
    loudness = shard_levels(rng, dims, cuts, -0.22, 0.18) if cuts else 1.0
    result = jax.random.normal(rng, dims, jnp.float32) * width * loudness
    return jnp.minimum(jnp.maximum(result, -limit), limit).astype(kind)


def setup_inputs(seed: int = 0, part: int = 0) -> dict:
    streams_of = jax.random.split(jax.random.key(seed), 7)
    part_keys = jax.random.split(jax.random.fold_in(streams_of[6], part), 7)
    tokens = bell_draw(part_keys[0], (TOKENS, D), 1.0, 6.0, ((0, 4), (1, 4)))
    expert_ids_keys = jax.random.split(jax.random.fold_in(part_keys[1], 1), TOKENS // TOK_DEV)
    expert_ids_turns = jax.random.permutation(jax.random.fold_in(part_keys[1], 3), TOKENS // TOK_DEV)
    expert_ids = jax.vmap(lambda own, number: routed_block(jax.random.fold_in(part_keys[1], 2), own, number, TOK_DEV, EXPERTS, 2, CAP, 2))(expert_ids_keys, expert_ids_turns).reshape((TOKENS, 2))
    router_logits = bell_draw(part_keys[2], (TOKENS, 2), 1.5, 6.0, ((0, 4),), jnp.float32)
    gate_weight = bell_draw(streams_of[3], (EXPERTS, D, FF), D ** -0.5, 0.109375, ((0, 4), (2, 4)))
    up_weight = bell_draw(streams_of[4], (EXPERTS, D, FF), D ** -0.5, 0.109375, ((0, 4), (2, 4)))
    down_weight = bell_draw(streams_of[5], (EXPERTS, FF, D), FF ** -0.5, 0.0625, ((0, 4), (1, 4)))
    return dict(tokens=tokens, expert_ids=expert_ids, router_logits=router_logits, gate_weight=gate_weight, up_weight=up_weight, down_weight=down_weight)


def route(ids, experts, cap):
    flat = ids.reshape(-1)
    onehot = (flat[:, None] == jnp.arange(experts, dtype=jnp.int32)[None, :]).astype(jnp.int32)
    before = jnp.cumsum(onehot, axis=0) - onehot
    slot = jnp.sum(before * onehot, axis=1)
    return (flat * cap + slot).reshape(ids.shape).astype(jnp.int32)


def placement_table(dest, slots_all):
    slot_ids = jnp.arange(slots_all, dtype=jnp.int32)[:, None]
    table = (slot_ids == dest[None, :, 0]).astype(jnp.float32) + (slot_ids == dest[None, :, 1]).astype(jnp.float32)
    return table.astype(jnp.bfloat16)


def expert_block(operands):
    rows, w_gate, w_up, w_down = operands
    gate = jnp.dot(rows, w_gate, preferred_element_type=jnp.float32)
    up = jnp.dot(rows, w_up, preferred_element_type=jnp.float32)
    hidden = (jax.nn.silu(gate) * up).astype(jnp.bfloat16)
    groups_h = hidden.reshape(hidden.shape[0], N_TENSOR, FF // N_TENSOR).transpose(1, 0, 2)
    groups_w = w_down.reshape(N_TENSOR, FF // N_TENSOR, D)

    def add_group(total, pair):
        part_h, part_w = pair
        partial_value = jnp.dot(part_h, part_w, preferred_element_type=jnp.float32).astype(jnp.bfloat16)
        return total + lax.optimization_barrier(partial_value).astype(jnp.float32), None

    total, unused = lax.scan(add_group, jnp.zeros((rows.shape[0], D), jnp.float32), (groups_h, groups_w))
    return total.astype(jnp.bfloat16)


def reference(tokens, expert_ids, router_logits, gate_weight, up_weight, down_weight):
    blocks = N_EXPERT
    dest = jax.vmap(lambda ids: route(ids, EXPERTS, CAP))(expert_ids.reshape(blocks, TOK_DEV, 2))
    x_blocks = tokens.reshape(blocks, TOK_DEV, D)

    def fill(dest_b, x_b):
        return jnp.dot(placement_table(dest_b, EXPERTS * CAP), x_b, preferred_element_type=jnp.float32).astype(jnp.bfloat16)

    buffers = jax.vmap(fill)(dest, x_blocks)
    rows = buffers.reshape(blocks, EXPERTS, CAP, D).transpose(1, 0, 2, 3).reshape(EXPERTS, blocks * CAP, D)
    expert_out = lax.map(expert_block, (rows, gate_weight, up_weight, down_weight))
    back = expert_out.reshape(EXPERTS, blocks, CAP, D).transpose(1, 0, 2, 3).reshape(blocks, EXPERTS * CAP, D)
    probs = jax.nn.softmax(router_logits.astype(jnp.float32), axis=-1).reshape(blocks, TOK_DEV, 2)
    picked = jax.vmap(lambda flat, d_b: jnp.take(flat, d_b, axis=0))(back, dest)
    mixed = jnp.sum(picked.astype(jnp.float32) * probs[..., None], axis=2)
    return mixed.reshape(TOKENS, D).astype(jnp.bfloat16)
```

```python
import functools

import jax
import jax.numpy as jnp
from jax import lax
from jax.experimental import pallas as pl
from jax.experimental.pallas import tpu as pltpu
from jax.sharding import PartitionSpec as P

MESH = pl.DeviceIdType.MESH
F32 = jnp.float32
BF16 = jnp.bfloat16
PAIRS = 4
CHUNKS = 2


def remote(src, dst, send_sem, recv_sem, device):
    return pltpu.make_async_remote_copy(
        src_ref=src,
        dst_ref=dst,
        send_sem=send_sem,
        recv_sem=recv_sem,
        device_id=device,
        device_id_type=MESH,
    )


def layer_kernel(
    meta_ref, tok_ref, gate_hbm, up_hbm, down_hbm, out_ref,
    metas, xg, place, blend, rows, acc, hidden, wgu, wdn, ybuf,
    give, keep, core_in, x_out, x_in, z_out, z_in,
    ms, mr, zs, zr, xs, xr, ss, sr, gsem, dsem, cs, cr, xs2, xr2, zs2, zr2,
):
    e = lax.axis_index("expert")
    z = lax.axis_index("tensor")
    x = e // 2
    c = e % 2
    sib = x * 2 + 1 - c
    opp = (1 - x) * 2 + c
    diag = (1 - x) * 2 + 1 - c
    zi = [z, z + 1 - 2 * (z % 2), (z + 2) % 4, 3 - z]
    tok_rows, width = tok_ref.shape
    half = tok_rows // 2
    ff = wgu.shape[3]
    nt = 256

    def gu_copies(s):
        i, j = s // 2, s % 2
        src = pl.ds(pl.multiple_of(zi[i] * width, width), width)
        slot = s % PAIRS
        return [
            pltpu.make_async_copy(gate_hbm.at[j, src, :], wgu.at[slot, 0], gsem.at[slot, 0]),
            pltpu.make_async_copy(up_hbm.at[j, src, :], wgu.at[slot, 1], gsem.at[slot, 1]),
        ]

    order = [2, 3, 1, 0]

    def down_copies(k):
        src = pl.ds(pl.multiple_of(zi[order[k]] * width, width), width)
        slot = k % CHUNKS
        return [
            pltpu.make_async_copy(down_hbm.at[j, :, src], wdn.at[slot, j], dsem.at[slot, j])
            for j in range(2)
        ]

    for s in range(PAIRS):
        for cp in gu_copies(s):
            cp.start()

    barrier = pltpu.get_barrier_semaphore()
    for peer in (sib, opp, diag):
        pl.semaphore_signal(barrier, inc=1, device_id={"expert": peer}, device_id_type=MESH)
    for i in (1, 2, 3):
        pl.semaphore_signal(barrier, inc=1, device_id={"tensor": zi[i]}, device_id_type=MESH)
    pl.semaphore_wait(barrier, 6)

    pending = []
    for n, peer in enumerate((sib, opp, diag)):
        cp = remote(meta_ref, metas.at[e], ms.at[n], mr.at[n], {"expert": peer})
        cp.start()
        pending.append(cp)

    def send_x(i, src):
        cp = remote(src, xg.at[zi[i], e], xs.at[i], xr.at[i], {"expert": opp})
        cp.start()
        pending.append(cp)

    def send_sib(kind, i, src, owner):
        cp = remote(src, xg.at[zi[i], owner], ss.at[kind, i], sr.at[kind, i], {"expert": sib})
        cp.start()
        pending.append(cp)

    send_x(0, tok_ref)
    for i in (1, 2, 3):
        cp = remote(tok_ref, xg.at[z, e], zs.at[i - 1], zr.at[i - 1], {"tensor": zi[i]})
        cp.start()
        pending.append(cp)
    send_sib(0, 0, tok_ref, e)

    for k in range(CHUNKS):
        for cp in down_copies(k):
            cp.start()

    xg[z, e] = tok_ref[...]
    metas[e] = meta_ref[...]

    def arrived_z(i):
        here = xg.at[zi[i], e]
        remote(here, here, zs.at[i - 1], zr.at[i - 1], {"tensor": zi[i]}).wait_recv()
        send_x(i, here)
        send_sib(0, i, here, e)

    def arrived_x(i):
        here = xg.at[zi[i], opp]
        remote(here, here, xs.at[i], xr.at[i], {"expert": opp}).wait_recv()
        send_sib(1, i, here, opp)

    def arrived_sib(i):
        for kind, owner in ((0, sib), (1, diag)):
            here = xg.at[zi[i], owner]
            remote(here, here, ss.at[kind, i], sr.at[kind, i], {"expert": sib}).wait_recv()

    for n, peer in enumerate((sib, opp, diag)):
        here = metas.at[peer]
        remote(here, here, ms.at[n], mr.at[n], {"expert": peer}).wait_recv()

    lane = lax.broadcasted_iota(jnp.int32, (tok_rows, tok_rows), 1)
    row = lax.broadcasted_iota(jnp.int32, (tok_rows, tok_rows), 0)
    earlier = (lane < row).astype(F32).astype(BF16)
    lane_f = lane.astype(F32)
    names = (lane + 2 * e).astype(F32)
    left = lane < half
    for b in range(4):
        cols = metas[b].T
        id0, id1 = cols[:, 0:1], cols[:, 1:2]
        l0, l1 = cols[:, 2:3], cols[:, 3:4]
        top = jnp.maximum(l0, l1)
        e0, e1 = jnp.exp(l0 - top), jnp.exp(l1 - top)
        total = e0 + e1
        hit0 = (id0 == names).astype(F32)
        hit1 = (id1 == names).astype(F32)
        named = hit0 + hit1
        prob = hit0 * (e0 / total) + hit1 * (e1 / total)
        before = jnp.dot(earlier, named.astype(BF16), preferred_element_type=F32)
        slot = jnp.where(left, before[:, 0:1], before[:, 1:2] + half)
        used = jnp.where(left, named[:, 0:1], named[:, 1:2])
        amount = jnp.where(left, prob[:, 0:1], prob[:, 1:2])
        same = (slot == lane_f).astype(F32)
        place[b] = (same * used).T.astype(BF16)
        blend[b] = (same * amount).astype(BF16)

    def fill(i):
        for b in range(4):
            got = jnp.dot(place[b], xg[zi[i], b], preferred_element_type=F32).astype(BF16)
            for j in range(2):
                rows[j, pl.ds(b * half, half), :] = got[j * half:(j + 1) * half]

    def gate_up(i, j):
        s = i * 2 + j
        slot = s % PAIRS
        for cp in gu_copies(s):
            cp.wait()

        def tile(n, carry):
            cols = pl.ds(pl.multiple_of(n * nt, nt), nt)
            g = jnp.dot(rows[j], wgu[slot, 0, :, cols], preferred_element_type=F32)
            u = jnp.dot(rows[j], wgu[slot, 1, :, cols], preferred_element_type=F32)
            if i > 0:
                g = g + acc[j, 0, :, cols]
                u = u + acc[j, 1, :, cols]
            if i < 3:
                acc[j, 0, :, cols] = g
                acc[j, 1, :, cols] = u
            else:
                hidden[j, :, cols] = (g / (1.0 + jnp.exp(-g)) * u).astype(BF16)
            return carry

        lax.fori_loop(0, ff // nt, tile, 0)
        if s + PAIRS < 8:
            for cp in gu_copies(s + PAIRS):
                cp.start()

    arrived_x(0)
    arrived_z(1)
    arrived_sib(0)
    fill(0)
    gate_up(0, 0)
    arrived_z(2)
    gate_up(0, 1)
    arrived_x(1)
    arrived_z(3)
    arrived_sib(1)
    fill(1)
    gate_up(1, 0)
    arrived_x(2)
    gate_up(1, 1)
    arrived_sib(2)
    fill(2)
    gate_up(2, 0)
    arrived_x(3)
    gate_up(2, 1)
    arrived_sib(3)
    fill(3)
    gate_up(3, 0)
    gate_up(3, 1)

    def down(k):
        slot = k % CHUNKS
        for cp in down_copies(k):
            cp.wait()

        def tile(n, carry):
            cols = pl.ds(pl.multiple_of(n * nt, nt), nt)
            for j in range(2):
                y = jnp.dot(hidden[j], wdn[slot, j, :, cols], preferred_element_type=F32).astype(BF16)
                for b in range(4):
                    ybuf[b, pl.ds(j * half, half), cols] = y[b * half:(b + 1) * half]
            return carry

        lax.fori_loop(0, width // nt, tile, 0)
        if k + CHUNKS < 4:
            for cp in down_copies(k + CHUNKS):
                cp.start()
        for at in range(2):
            b = at * 2 + 1 - c
            give[k, at] = jnp.dot(blend[b], ybuf[b], preferred_element_type=F32).astype(BF16)
        cp = remote(give.at[k], core_in.at[k], cs.at[k], cr.at[k], {"expert": sib})
        cp.start()
        pending.append(cp)
        for at in range(2):
            b = at * 2 + c
            keep[k, at] = jnp.dot(blend[b], ybuf[b], preferred_element_type=F32).astype(BF16)

    def over_x(k):
        here = core_in.at[k]
        remote(here, here, cs.at[k], cr.at[k], {"expert": sib}).wait_recv()
        x_out[k] = (keep[k, 1 - x].astype(F32) + core_in[k, 1 - x].astype(F32)).astype(BF16)
        cp = remote(x_out.at[k], x_in.at[k], xs2.at[k], xr2.at[k], {"expert": opp})
        cp.start()
        pending.append(cp)

    def summed(k):
        here = x_in.at[k]
        remote(here, here, xs2.at[k], xr2.at[k], {"expert": opp}).wait_recv()
        return keep[k, x].astype(F32) + core_in[k, x].astype(F32) + x_in[k].astype(F32)

    def over_z(k):
        i = order[k]
        z_out[k] = summed(k).astype(BF16)
        cp = remote(z_out.at[k], z_in.at[k], zs2.at[k], zr2.at[k], {"tensor": zi[i]})
        cp.start()
        pending.append(cp)

    for k in range(4):
        down(k)
        over_x(k)
        if k:
            over_z(k - 1)
    mine = summed(3)
    for k in range(3):
        here = z_in.at[k]
        remote(here, here, zs2.at[k], zr2.at[k], {"tensor": zi[order[k]]}).wait_recv()
        mine = mine + z_in[k].astype(F32)
    out_ref[...] = mine.astype(BF16)
    for cp in pending:
        cp.wait_send()


def fused(tokens, expert_ids, router_logits, gate_weight, up_weight, down_weight):
    tok_rows, width = tokens.shape
    ff = gate_weight.shape[2]
    half = tok_rows // 2
    slots = 4 * half
    meta = jnp.concatenate(
        [expert_ids.T.astype(F32), router_logits.T, jnp.zeros((4, tok_rows), F32)], axis=0
    )
    vmem = pl.BlockSpec(memory_space=pltpu.VMEM)
    anywhere = pl.BlockSpec(memory_space=pl.ANY)
    dma = pltpu.SemaphoreType.DMA
    flops = 2 * 2 * slots * 3 * (4 * width) * ff
    return pl.pallas_call(
        layer_kernel,
        out_shape=jax.ShapeDtypeStruct((tok_rows, width), BF16),
        in_specs=[vmem, vmem, anywhere, anywhere, anywhere],
        out_specs=vmem,
        scratch_shapes=[
            pltpu.VMEM((4, 8, tok_rows), F32),
            pltpu.VMEM((4, 4, tok_rows, width), BF16),
            pltpu.VMEM((4, tok_rows, tok_rows), BF16),
            pltpu.VMEM((4, tok_rows, tok_rows), BF16),
            pltpu.VMEM((2, slots, width), BF16),
            pltpu.VMEM((2, 2, slots, ff), F32),
            pltpu.VMEM((2, slots, ff), BF16),
            pltpu.VMEM((PAIRS, 2, width, ff), BF16),
            pltpu.VMEM((CHUNKS, 2, ff, width), BF16),
            pltpu.VMEM((4, tok_rows, width), BF16),
            pltpu.VMEM((4, 2, tok_rows, width), BF16),
            pltpu.VMEM((4, 2, tok_rows, width), BF16),
            pltpu.VMEM((4, 2, tok_rows, width), BF16),
            pltpu.VMEM((4, tok_rows, width), BF16),
            pltpu.VMEM((4, tok_rows, width), BF16),
            pltpu.VMEM((3, tok_rows, width), BF16),
            pltpu.VMEM((3, tok_rows, width), BF16),
            dma((3,)), dma((3,)), dma((3,)), dma((3,)), dma((4,)), dma((4,)),
            dma((2, 4)), dma((2, 4)), dma((PAIRS, 2)), dma((CHUNKS, 2)),
            dma((4,)), dma((4,)), dma((4,)), dma((4,)), dma((3,)), dma((3,)),
        ],
        compiler_params=pltpu.CompilerParams(
            collective_id=0, has_side_effects=True, vmem_limit_bytes=64 * 1024 * 1024
        ),
        cost_estimate=pl.CostEstimate(
            flops=flops, bytes_accessed=12 * 4 * width * ff, transcendentals=2 * slots * ff
        ),
    )(meta, tokens, gate_weight, up_weight, down_weight)


def route(ids, experts, cap):
    flat = ids.reshape(-1)
    onehot = (flat[:, None] == jnp.arange(experts, dtype=jnp.int32)[None, :]).astype(jnp.int32)
    before = jnp.cumsum(onehot, axis=0) - onehot
    slot = jnp.sum(before * onehot, axis=1)
    return (flat * cap + slot).reshape(ids.shape)


def placement_table(dest, slots_all):
    slot_ids = jnp.arange(slots_all, dtype=jnp.int32)[:, None]
    table = (slot_ids == dest[None, :, 0]).astype(jnp.float32) + (
        slot_ids == dest[None, :, 1]
    ).astype(jnp.float32)
    return table.astype(jnp.bfloat16)


def on_device(tokens, expert_ids, router_logits, gate_weight, up_weight, down_weight):
    tok_rows = tokens.shape[0]
    local_experts = gate_weight.shape[0]
    experts = local_experts * lax.axis_size("expert")
    cap = tok_rows // 2
    dest = route(expert_ids, experts, cap)
    table = placement_table(dest, experts * cap)
    whole = lax.all_gather(tokens, "tensor", axis=1, tiled=True)
    buffer = jnp.dot(table, whole, preferred_element_type=jnp.float32).astype(jnp.bfloat16)
    buffer = buffer.reshape(experts, 1, cap, whole.shape[1])
    arrived = lax.all_to_all(buffer, "expert", split_axis=0, concat_axis=1, tiled=True)
    rows = arrived.reshape(local_experts, -1, whole.shape[1])
    gate = jnp.einsum("erd,edf->erf", rows, gate_weight, preferred_element_type=jnp.float32)
    up = jnp.einsum("erd,edf->erf", rows, up_weight, preferred_element_type=jnp.float32)
    hidden = (jax.nn.silu(gate) * up).astype(jnp.bfloat16)
    terms = jnp.einsum("erf,efd->erd", hidden, down_weight, preferred_element_type=jnp.float32)
    share = lax.psum_scatter(terms.astype(jnp.bfloat16), "tensor", scatter_dimension=2, tiled=True)
    width_dev = share.shape[2]
    share = share.reshape(local_experts, -1, cap, width_dev)
    back = lax.all_to_all(share, "expert", split_axis=1, concat_axis=0, tiled=True)
    flat = back.reshape(experts * cap, width_dev)
    probs = jax.nn.softmax(router_logits, axis=-1)
    picked = jnp.take(flat, dest, axis=0)
    mixed = jnp.sum(picked.astype(jnp.float32) * probs[..., None], axis=1)
    return mixed.astype(jnp.bfloat16)


def solution(mesh):
    placed = (
        P(("groups", "expert"), "tensor"),
        P(("groups", "expert"), None),
        P(("groups", "expert"), None),
        P("expert", None, "tensor"),
        P("expert", None, "tensor"),
        P("expert", "tensor", None),
    )
    sizes = (mesh.shape["expert"], mesh.shape["tensor"])

    def per_device(*args):
        tokens, gate_weight = args[0], args[3]
        fits = sizes == (4, 4) and gate_weight.shape[0] == 2 and tokens.shape[1] % 256 == 0
        fits = fits and tokens.shape[0] == 128 and gate_weight.shape[2] % 256 == 0
        return (fused if fits else on_device)(*args)

    return jax.shard_map(
        per_device,
        mesh=mesh,
        in_specs=placed,
        out_specs=P(("groups", "expert"), "tensor"),
        check_vma=False,
    )
```

```python
import functools

import jax
import jax.numpy as jnp
from jax import lax
from jax.experimental import pallas as pl
from jax.experimental.pallas import tpu as pltpu
from jax.sharding import PartitionSpec as P

MESH = pl.DeviceIdType.MESH
F32 = jnp.float32
BF16 = jnp.bfloat16
PAIRS = 4
CHUNKS = 2


def remote(src, dst, send_sem, recv_sem, device):
    return pltpu.make_async_remote_copy(
        src_ref=src,
        dst_ref=dst,
        send_sem=send_sem,
        recv_sem=recv_sem,
        device_id=device,
        device_id_type=MESH,
    )


def layer_kernel(
    meta_ref, tok_ref, gate_hbm, up_hbm, down_hbm, out_ref,
    metas, xg, place, blend, rows, acc, hidden, wgu, wdn, ybuf,
    give, keep, core_in, x_out, x_in, z_out, z_in,
    ms, mr, zs, zr, xs, xr, ss, sr, gsem, dsem, cs, cr, xs2, xr2, zs2, zr2,
):
    e = lax.axis_index("expert")
    z = lax.axis_index("tensor")
    x = e // 2
    c = e % 2
    sib = x * 2 + 1 - c
    opp = (1 - x) * 2 + c
    diag = (1 - x) * 2 + 1 - c
    mate, other = z + 1 - 2 * (z % 2), 3 - z
    zi = [z, mate, 2 - z // 2, 3 * (1 - z // 2)]
    inner = (z + 1) // 2 == 1
    end = (z + 1) // 2 != 1
    tok_rows, width = tok_ref.shape
    half = tok_rows // 2
    ff = wgu.shape[3]
    nt = ff // 2

    def gu_copies(s):
        i, j = s // 2, s % 2
        src = pl.ds(pl.multiple_of(zi[i] * width, width), width)
        slot = s % PAIRS
        return [
            pltpu.make_async_copy(gate_hbm.at[j, src, :], wgu.at[slot, 0], gsem.at[slot, 0]),
            pltpu.make_async_copy(up_hbm.at[j, src, :], wgu.at[slot, 1], gsem.at[slot, 1]),
        ]

    order = [3, 2, 1, 0]

    def down_copies(k):
        src = pl.ds(pl.multiple_of(zi[order[k]] * width, width), width)
        slot = k % CHUNKS
        return [
            pltpu.make_async_copy(down_hbm.at[j, :, src], wdn.at[slot, j], dsem.at[slot, j])
            for j in range(2)
        ]

    for s in range(PAIRS):
        for cp in gu_copies(s):
            cp.start()

    barrier = pltpu.get_barrier_semaphore()
    for peer in (sib, opp, diag):
        pl.semaphore_signal(barrier, inc=1, device_id={"expert": peer}, device_id_type=MESH)
    pl.semaphore_signal(barrier, inc=1, device_id={"tensor": mate}, device_id_type=MESH)

    @pl.when(inner)
    def _():
        pl.semaphore_signal(barrier, inc=1, device_id={"tensor": other}, device_id_type=MESH)
        pl.semaphore_wait(barrier, 5)

    @pl.when(end)
    def _():
        pl.semaphore_wait(barrier, 4)


    pending = []
    for n, peer in enumerate((sib, opp, diag)):
        cp = remote(meta_ref, metas.at[e], ms.at[n], mr.at[n], {"expert": peer})
        cp.start()
        pending.append(cp)

    def send_x(i, src):
        cp = remote(src, xg.at[zi[i], e], xs.at[i], xr.at[i], {"expert": opp})
        cp.start()
        pending.append(cp)

    def send_sib(kind, i, src, owner):
        cp = remote(src, xg.at[zi[i], owner], ss.at[kind, i], sr.at[kind, i], {"expert": sib})
        cp.start()
        pending.append(cp)

    send_x(0, tok_ref)
    pending_inner = []

    def send_z(n, src, shard, peer, only_inner):
        cp = remote(src, xg.at[shard, e], zs.at[n], zr.at[shard], {"tensor": peer})
        if only_inner:
            pl.when(inner)(cp.start)
            pending_inner.append(cp)
        else:
            cp.start()
            pending.append(cp)

    send_z(0, tok_ref, z, mate, False)
    send_z(1, tok_ref, z, other, True)
    send_sib(0, 0, tok_ref, e)

    for k in range(CHUNKS):
        for cp in down_copies(k):
            cp.start()

    xg[z, e] = tok_ref[...]
    metas[e] = meta_ref[...]

    def arrived_z(i):
        here = xg.at[zi[i], e]
        remote(here, here, zs.at[0], zr.at[zi[i]], {"tensor": mate}).wait_recv()
        send_z(i + 1, here, zi[i], other if i == 1 else mate, True)
        send_x(i, here)
        send_sib(0, i, here, e)

    def arrived_x(i):
        here = xg.at[zi[i], opp]
        remote(here, here, xs.at[i], xr.at[i], {"expert": opp}).wait_recv()
        send_sib(1, i, here, opp)

    def arrived_sib(i):
        for kind, owner in ((0, sib), (1, diag)):
            here = xg.at[zi[i], owner]
            remote(here, here, ss.at[kind, i], sr.at[kind, i], {"expert": sib}).wait_recv()

    for n, peer in enumerate((sib, opp, diag)):
        here = metas.at[peer]
        remote(here, here, ms.at[n], mr.at[n], {"expert": peer}).wait_recv()

    lane = lax.broadcasted_iota(jnp.int32, (tok_rows, tok_rows), 1)
    row = lax.broadcasted_iota(jnp.int32, (tok_rows, tok_rows), 0)
    earlier = (lane < row).astype(F32).astype(BF16)
    lane_f = lane.astype(F32)
    names = (lane + 2 * e).astype(F32)
    left = lane < half
    for b in range(4):
        cols = metas[b].T
        id0, id1 = cols[:, 0:1], cols[:, 1:2]
        l0, l1 = cols[:, 2:3], cols[:, 3:4]
        top = jnp.maximum(l0, l1)
        e0, e1 = jnp.exp(l0 - top), jnp.exp(l1 - top)
        total = e0 + e1
        hit0 = (id0 == names).astype(F32)
        hit1 = (id1 == names).astype(F32)
        named = hit0 + hit1
        prob = hit0 * (e0 / total) + hit1 * (e1 / total)
        before = jnp.dot(earlier, named.astype(BF16), preferred_element_type=F32)
        slot = jnp.where(left, before[:, 0:1], before[:, 1:2] + half)
        used = jnp.where(left, named[:, 0:1], named[:, 1:2])
        amount = jnp.where(left, prob[:, 0:1], prob[:, 1:2])
        same = (slot == lane_f).astype(F32)
        place[b] = (same * used).T.astype(BF16)
        blend[b] = (same * amount).astype(BF16)

    def fill(i):
        for b in range(4):
            got = jnp.dot(place[b], xg[zi[i], b], preferred_element_type=F32).astype(BF16)
            for j in range(2):
                rows[j, pl.ds(b * half, half), :] = got[j * half:(j + 1) * half]

    def gate_up(i, j):
        s = i * 2 + j
        slot = s % PAIRS
        for cp in gu_copies(s):
            cp.wait()

        def tile(n, carry):
            cols = pl.ds(pl.multiple_of(n * nt, nt), nt)
            g = jnp.dot(rows[j], wgu[slot, 0, :, cols], preferred_element_type=F32)
            if i > 0:
                g = g + acc[j, 0, :, cols]
            if i < 3:
                acc[j, 0, :, cols] = g
            u = jnp.dot(rows[j], wgu[slot, 1, :, cols], preferred_element_type=F32)
            if i > 0:
                u = u + acc[j, 1, :, cols]
            if i < 3:
                acc[j, 1, :, cols] = u
            else:
                hidden[j, :, cols] = (g / (1.0 + jnp.exp(-g)) * u).astype(BF16)
            return carry

        lax.fori_loop(0, ff // nt, tile, 0)
        if s + PAIRS < 8:
            for cp in gu_copies(s + PAIRS):
                cp.start()

    arrived_x(0)
    arrived_z(1)
    arrived_sib(0)
    fill(0)
    gate_up(0, 0)
    arrived_z(2)
    gate_up(0, 1)
    arrived_x(1)
    arrived_z(3)
    arrived_sib(1)
    fill(1)
    gate_up(1, 0)
    arrived_x(2)
    gate_up(1, 1)
    arrived_sib(2)
    fill(2)
    gate_up(2, 0)
    arrived_x(3)
    gate_up(2, 1)
    arrived_sib(3)
    fill(3)
    gate_up(3, 0)
    gate_up(3, 1)

    def down(k):
        slot = k % CHUNKS
        for cp in down_copies(k):
            cp.wait()

        for n in range(0, width, 256):
            cols = slice(n, n + 256)
            for j in range(2):
                y = jnp.dot(hidden[j], wdn[slot, j, :, cols], preferred_element_type=F32).astype(BF16)
                for b in range(4):
                    ybuf[b, pl.ds(j * half, half), cols] = y[b * half:(b + 1) * half]
        if k + CHUNKS < 4:
            for cp in down_copies(k + CHUNKS):
                cp.start()
        for at in range(2):
            b = at * 2 + 1 - c
            give[k, at] = jnp.dot(blend[b], ybuf[b], preferred_element_type=F32).astype(BF16)
        cp = remote(give.at[k], core_in.at[k], cs.at[k], cr.at[k], {"expert": sib})
        cp.start()
        pending.append(cp)
        for at in range(2):
            b = at * 2 + c
            keep[k, at] = jnp.dot(blend[b], ybuf[b], preferred_element_type=F32).astype(BF16)

    def over_x(k):
        here = core_in.at[k]
        remote(here, here, cs.at[k], cr.at[k], {"expert": sib}).wait_recv()
        x_out[k] = (keep[k, 1 - x].astype(F32) + core_in[k, 1 - x].astype(F32)).astype(BF16)
        cp = remote(x_out.at[k], x_in.at[k], xs2.at[k], xr2.at[k], {"expert": opp})
        cp.start()
        pending.append(cp)

    def summed(k):
        here = x_in.at[k]
        remote(here, here, xs2.at[k], xr2.at[k], {"expert": opp}).wait_recv()
        return keep[k, x].astype(F32) + core_in[k, x].astype(F32) + x_in[k].astype(F32)

    def z_copy(k, slot, peer):
        return remote(z_out.at[k], z_in.at[slot], zs2.at[k], zr2.at[slot], {"tensor": peer})

    def z_arrived(slot):
        here = z_in.at[slot]
        remote(here, here, zs2.at[0], zr2.at[slot], {"tensor": mate}).wait_recv()
        return z_in[slot].astype(F32)

    def end_z(k):
        @pl.when(end)
        def _():
            z_out[k] = summed(k).astype(BF16)
            z_copy(k, (0, 1, 3)[k], mate).start()

    def inner_z(k):
        @pl.when(inner)
        def _():
            z_out[k] = (summed(k) + z_arrived(k)).astype(BF16)
            z_copy(k, (2, 4, 3)[k], mate if k == 2 else other).start()

    down(0)
    over_x(0)
    down(1)
    over_x(1)
    end_z(0)
    down(2)
    over_x(2)
    inner_z(0)
    end_z(1)
    down(3)
    over_x(3)
    inner_z(1)
    end_z(2)
    inner_z(2)
    mine = summed(3) + z_arrived(3)

    @pl.when(end)
    def _():
        out_ref[...] = mine.astype(BF16)

    @pl.when(inner)
    def _():
        out_ref[...] = (mine + z_arrived(4)).astype(BF16)

    for k in range(3):
        z_copy(k, 3, mate).wait_send()
    for cp in pending_inner:
        pl.when(inner)(cp.wait_send)
    for cp in pending:
        cp.wait_send()


def fused(tokens, expert_ids, router_logits, gate_weight, up_weight, down_weight):
    tok_rows, width = tokens.shape
    ff = gate_weight.shape[2]
    half = tok_rows // 2
    slots = 4 * half
    meta = jnp.concatenate(
        [expert_ids.T.astype(F32), router_logits.T, jnp.zeros((4, tok_rows), F32)], axis=0
    )
    vmem = pl.BlockSpec(memory_space=pltpu.VMEM)
    anywhere = pl.BlockSpec(memory_space=pl.ANY)
    dma = pltpu.SemaphoreType.DMA
    flops = 2 * 2 * slots * 3 * (4 * width) * ff
    return pl.pallas_call(
        layer_kernel,
        out_shape=jax.ShapeDtypeStruct((tok_rows, width), BF16),
        in_specs=[vmem, vmem, anywhere, anywhere, anywhere],
        out_specs=vmem,
        scratch_shapes=[
            pltpu.VMEM((4, 8, tok_rows), F32),
            pltpu.VMEM((4, 4, tok_rows, width), BF16),
            pltpu.VMEM((4, tok_rows, tok_rows), BF16),
            pltpu.VMEM((4, tok_rows, tok_rows), BF16),
            pltpu.VMEM((2, slots, width), BF16),
            pltpu.VMEM((2, 2, slots, ff), F32),
            pltpu.VMEM((2, slots, ff), BF16),
            pltpu.VMEM((PAIRS, 2, width, ff), BF16),
            pltpu.VMEM((CHUNKS, 2, ff, width), BF16),
            pltpu.VMEM((4, tok_rows, width), BF16),
            pltpu.VMEM((4, 2, tok_rows, width), BF16),
            pltpu.VMEM((4, 2, tok_rows, width), BF16),
            pltpu.VMEM((4, 2, tok_rows, width), BF16),
            pltpu.VMEM((4, tok_rows, width), BF16),
            pltpu.VMEM((4, tok_rows, width), BF16),
            pltpu.VMEM((3, tok_rows, width), BF16),
            pltpu.VMEM((5, tok_rows, width), BF16),
            dma((3,)), dma((3,)), dma((5,)), dma((4,)), dma((4,)), dma((4,)),
            dma((2, 4)), dma((2, 4)), dma((PAIRS, 2)), dma((CHUNKS, 2)),
            dma((4,)), dma((4,)), dma((4,)), dma((4,)), dma((3,)), dma((5,)),
        ],
        compiler_params=pltpu.CompilerParams(
            collective_id=0, has_side_effects=True, vmem_limit_bytes=64 * 1024 * 1024
        ),
        cost_estimate=pl.CostEstimate(
            flops=flops, bytes_accessed=12 * 4 * width * ff, transcendentals=2 * slots * ff
        ),
    )(meta, tokens, gate_weight, up_weight, down_weight)


def route(ids, experts, cap):
    flat = ids.reshape(-1)
    onehot = (flat[:, None] == jnp.arange(experts, dtype=jnp.int32)[None, :]).astype(jnp.int32)
    before = jnp.cumsum(onehot, axis=0) - onehot
    slot = jnp.sum(before * onehot, axis=1)
    return (flat * cap + slot).reshape(ids.shape)


def placement_table(dest, slots_all):
    slot_ids = jnp.arange(slots_all, dtype=jnp.int32)[:, None]
    table = (slot_ids == dest[None, :, 0]).astype(jnp.float32) + (
        slot_ids == dest[None, :, 1]
    ).astype(jnp.float32)
    return table.astype(jnp.bfloat16)


def on_device(tokens, expert_ids, router_logits, gate_weight, up_weight, down_weight):
    tok_rows = tokens.shape[0]
    local_experts = gate_weight.shape[0]
    experts = local_experts * lax.axis_size("expert")
    cap = tok_rows // 2
    dest = route(expert_ids, experts, cap)
    table = placement_table(dest, experts * cap)
    whole = lax.all_gather(tokens, "tensor", axis=1, tiled=True)
    buffer = jnp.dot(table, whole, preferred_element_type=jnp.float32).astype(jnp.bfloat16)
    buffer = buffer.reshape(experts, 1, cap, whole.shape[1])
    arrived = lax.all_to_all(buffer, "expert", split_axis=0, concat_axis=1, tiled=True)
    rows = arrived.reshape(local_experts, -1, whole.shape[1])
    gate = jnp.einsum("erd,edf->erf", rows, gate_weight, preferred_element_type=jnp.float32)
    up = jnp.einsum("erd,edf->erf", rows, up_weight, preferred_element_type=jnp.float32)
    hidden = (jax.nn.silu(gate) * up).astype(jnp.bfloat16)
    terms = jnp.einsum("erf,efd->erd", hidden, down_weight, preferred_element_type=jnp.float32)
    share = lax.psum_scatter(terms.astype(jnp.bfloat16), "tensor", scatter_dimension=2, tiled=True)
    width_dev = share.shape[2]
    share = share.reshape(local_experts, -1, cap, width_dev)
    back = lax.all_to_all(share, "expert", split_axis=1, concat_axis=0, tiled=True)
    flat = back.reshape(experts * cap, width_dev)
    probs = jax.nn.softmax(router_logits, axis=-1)
    picked = jnp.take(flat, dest, axis=0)
    mixed = jnp.sum(picked.astype(jnp.float32) * probs[..., None], axis=1)
    return mixed.astype(jnp.bfloat16)


def solution(mesh):
    placed = (
        P(("groups", "expert"), "tensor"),
        P(("groups", "expert"), None),
        P(("groups", "expert"), None),
        P("expert", None, "tensor"),
        P("expert", None, "tensor"),
        P("expert", "tensor", None),
    )
    sizes = (mesh.shape["expert"], mesh.shape["tensor"])

    def per_device(*args):
        tokens, gate_weight = args[0], args[3]
        fits = sizes == (4, 4) and gate_weight.shape[0] == 2 and tokens.shape[1] % 256 == 0
        fits = fits and tokens.shape[0] == 128 and gate_weight.shape[2] % 512 == 0
        return (fused if fits else on_device)(*args)

    return jax.shard_map(
        per_device,
        mesh=mesh,
        in_specs=placed,
        out_specs=P(("groups", "expert"), "tensor"),
        check_vma=False,
    )
```
